32 devices in a mesh: leaf: 4 (over y, x), blk: 8 (over z, core).
Axes of the slice: x: 2, y: 2, z: 4, core: 2. Of those that a mesh axis runs over, the one named last changes fastest.
Arguments:
- near_tiles: bfloat16 [32, 8, 512, 512], P('leaf', 'blk'), may hold values from -0.25 to 0.25
- near_cols: int32 [32, 8], P('leaf', 'blk'), may hold values from 0 to 31, as said below
- near_count: int32 [32], P('leaf'), may hold values from 1 to 8, as said below
- probes: bfloat16 [32, 512, 512], P('leaf'), may hold values from -6 to 6
- mixing: float32 [512, 64], replicated, may hold values from -0.25 to 0.25
- far_tiles: bfloat16 [32, 8, 512, 512], P('leaf', 'blk'), may hold values from -6 to 6
- far_cols: int32 [32, 8], P('leaf', 'blk'), may hold values from 0 to 31, as said below
Outputs:
- coupling: float32 [32, 8, 64, 64], P('leaf', 'blk')
- root_part: float32 [32, 64, 64], P('leaf')
The draws below stay inside these ranges and needn't reach their ends.
Inputs may be any that keep to these rules, and one draw needn't show every extreme that they name: near_cols[r, k] lies within 8 of r; the slots below near_count[r] name distinct clusters. Slots at or past near_count[r] hold arbitrary tiles that must be ignored. far_cols[r, j] differs from r by more than 8.
All inputs are finite; a program needn't handle non-finite values.
Results may differ from the reference program's by a relative error of at most 0.0041.
Values may be sent and summed in bfloat16 or wider, within the bound.
A program may use at most 128 MiB of HBM per device.

```python
import math
import jax
import jax.numpy as jnp
from jax import lax

B = 512
RANK = 64
P_SIZE = 512
RC_DEV = 8
REACH = 8
CLUSTERS = 32
NEAR = 8
FAR = 8
N_LEAF = 4


def draw_near_cols(key, part):
    window_size = 2 * REACH + 1
    offsets = jnp.arange(window_size) - REACH
    row_ids = jnp.arange(CLUSTERS)[:, None]
    target = row_ids + offsets[None, :]
    inside = (target >= 0) & (target < CLUSTERS)
    scores = jax.random.randint(key, (CLUSTERS, window_size), 0, 1 << 20) * 64 + jnp.arange(window_size)[None, :]
    scores = jnp.where(inside, scores, scores + (1 << 27))
    ordering = jnp.argsort(scores, axis=1, stable=True)[:, :NEAR]
    picked = jnp.take_along_axis(target, ordering, axis=1)
    return jnp.clip(picked, 0, CLUSTERS - 1).astype(jnp.int32)


def draw_near_count(key, part):
    first_key, second_key, third_key = jax.random.split(key, 3)
    row_ids = jnp.arange(CLUSTERS)
    base_count = jax.random.randint(first_key, (CLUSTERS,), 1, NEAR // 2 + 1)
    dense_count = jax.random.randint(second_key, (CLUSTERS,), 3 * NEAR // 4, NEAR + 1)
    dense_start = jax.random.randint(third_key, (), REACH, CLUSTERS - REACH - CLUSTERS // 4 + 1)
    inside = (row_ids >= dense_start) & (row_ids < dense_start + CLUSTERS // 4)
    counts = jnp.where(inside, dense_count, base_count)
    counts = jnp.where(row_ids == dense_start, NEAR, counts)
    valid_count = jnp.minimum(row_ids, REACH) + jnp.minimum(CLUSTERS - 1 - row_ids, REACH) + 1
    return jnp.minimum(counts, valid_count).astype(jnp.int32)


def draw_far_cols(key, part):
    row_ids = jnp.arange(CLUSTERS)[:, None]
    distance = jax.random.randint(key, (CLUSTERS, FAR), REACH + 1, CLUSTERS - REACH)
    return ((row_ids + distance) % CLUSTERS).astype(jnp.int32)


def block_scale(own_key, extent, cuts, smallest, largest):
    def one(position, blocks):
        draws = jax.random.uniform(jax.random.fold_in(jax.random.fold_in(own_key, 6), position), (blocks,), jnp.float32, smallest / len(cuts), largest / len(cuts))
        return jnp.repeat(jnp.exp(draws), extent[position] // blocks).reshape((-1,) + (1,) * (len(extent) - position - 1))

    level = one(*cuts[0])
    for cut in cuts[1:]:
        level = level * one(*cut)
    return level


def gaussian(rng, extent, spread, bound, pieces=(), kind=jnp.bfloat16):
    array = spread * jax.random.normal(rng, extent, jnp.float32)
    if pieces:
        array = array * block_scale(rng, extent, pieces, -0.22, 0.18)
    return jnp.clip(array, -bound, bound).astype(kind)


def setup_inputs(seed: int = 0) -> dict:
    key_list = jax.random.split(jax.random.key(seed), 8)
    near_tiles = gaussian(key_list[0], (CLUSTERS, NEAR, B, B), B ** -0.5, 0.25, ((0, 4), (1, 8)))
    near_cols = draw_near_cols(jax.random.fold_in(key_list[7], 71), 0)
    near_count = draw_near_count(jax.random.fold_in(key_list[7], 71), 0)
    probes = gaussian(key_list[3], (CLUSTERS, B, P_SIZE), 1.0, 6.0, ((0, 4),))
    mixing = gaussian(key_list[4], (P_SIZE, RANK), P_SIZE ** -0.5, 0.25, (), jnp.float32)
    far_tiles = gaussian(key_list[5], (CLUSTERS, FAR, B, B), 1.0, 6.0, ((0, 4), (1, 8)))
    far_cols = draw_far_cols(jax.random.fold_in(key_list[7], 71), 0)
    return dict(near_tiles=near_tiles, near_cols=near_cols, near_count=near_count, probes=probes, mixing=mixing, far_tiles=far_tiles, far_cols=far_cols)


highest = lax.Precision.HIGHEST

def basis_from(gram_matrix, mixed_rows):
    lower_factor = jnp.linalg.cholesky(gram_matrix)
    solved = jax.scipy.linalg.solve_triangular(lower_factor, jnp.swapaxes(mixed_rows, -1, -2), lower=True)
    return jnp.swapaxes(solved, -1, -2)

def merge(stacked, mixing):
    mixed_rows = jnp.einsum('...mp,pk->...mk', stacked, mixing, precision=highest)
    gram_matrix = jnp.einsum('...mk,...ml->...kl', mixed_rows, mixed_rows, precision=highest)
    transfer = basis_from(gram_matrix, mixed_rows)
    merged = jnp.einsum('...mk,...mp->...kp', transfer, stacked, precision=highest)
    return (transfer, merged)

def reference(near_tiles, near_cols, near_count, probes, mixing, far_tiles, far_cols):
    slot_ids = jnp.arange(near_cols.shape[1])

    def leaf_sketch(operands):
        row_tiles, row_cols, row_count = operands
        gathered = probes[row_cols].astype(jnp.float32)
        products = jnp.einsum('kab,kbp->kap', row_tiles.astype(jnp.float32), gathered)
        keep_mask = (slot_ids < row_count).astype(products.dtype)
        return jnp.einsum('k,kap->ap', keep_mask, products)
    sketch = lax.map(leaf_sketch, (near_tiles, near_cols, near_count))
    compressed = jnp.einsum('rbp,pk->rbk', sketch, mixing, precision=highest)
    gram_matrix = jnp.einsum('rbk,rbl->rkl', compressed, compressed, precision=highest)
    leaf_basis = basis_from(gram_matrix, compressed)
    leaf_proj = jnp.einsum('rbk,rbp->rkp', leaf_basis, sketch, precision=highest)
    basis_low = leaf_basis.astype(jnp.bfloat16)

    def couple(operands):
        row_tiles, row_cols, own_basis = operands
        far_image = jnp.einsum('jab,jbk->jak', row_tiles.astype(jnp.float32), basis_low[row_cols].astype(jnp.float32))
        return jnp.einsum('ak,jal->jkl', own_basis.astype(jnp.float32), far_image, precision=highest)
    coupling = lax.map(couple, (far_tiles, far_cols, basis_low))
    sub_stack = leaf_proj.reshape(N_LEAF, RC_DEV * RANK, leaf_proj.shape[2])
    sub_transfer, node_sketches = merge(sub_stack, mixing)
    levels = N_LEAF.bit_length() - 1
    path_factor = jnp.broadcast_to(jnp.eye(RANK, dtype=jnp.float32), (N_LEAF, RANK, RANK))
    subtree_ids = jnp.arange(N_LEAF)
    for depth_index in range(levels):
        paired = node_sketches.reshape(node_sketches.shape[0] // 2, 2 * RANK, node_sketches.shape[2])
        transfer, node_sketches = merge(paired, mixing)
        halves = transfer.reshape(transfer.shape[0], 2, RANK, RANK)
        picked = halves[subtree_ids >> depth_index + 1, subtree_ids >> depth_index & 1]
        path_factor = jnp.einsum('gab,gbc->gac', path_factor, picked, precision=highest)
    sub_blocks = sub_transfer.reshape(N_LEAF, RC_DEV, RANK, RANK)
    root_part = jnp.einsum('gcab,gbd->gcad', sub_blocks, path_factor, precision=highest)
    root_part = root_part.reshape(N_LEAF * RC_DEV, RANK, RANK) * math.sqrt(N_LEAF * RC_DEV * RANK)
    return (coupling, root_part)
```

```python
import functools
import math

import jax
import jax.numpy as jnp
from jax import lax
from jax.experimental import pallas as pl
from jax.experimental.pallas import tpu as pltpu
from jax.sharding import PartitionSpec as P

REACH = 8
MESH = pl.DeviceIdType.MESH
highest = lax.Precision.HIGHEST
f32 = jnp.float32
bf16 = jnp.bfloat16


def split_terms(value):
    high = value.astype(bf16)
    low = (value - high.astype(f32)).astype(bf16)
    return jnp.concatenate([high, low], axis=1)


def factor(gram):
    rank = gram.shape[0]
    rows = lax.broadcasted_iota(jnp.int32, (rank, 2 * rank), 0)
    lanes = lax.broadcasted_iota(jnp.int32, (rank, 2 * rank), 1)
    unit = jnp.where(lanes - rank == rows, 1.0, 0.0).astype(f32)
    work = jnp.where(lanes < rank, jnp.concatenate([gram, gram], axis=1), unit)
    done = []
    for start in range(0, rank, 8):
        index = lax.broadcasted_iota(jnp.int32, work.shape, 0)
        for step in range(8):
            j = start + step
            row = work[step : step + 1, :]
            inverse = 1.0 / work[step : step + 1, j : j + 1]
            column = work[:, j : j + 1]
            work = work - jnp.where(index > step, column * (row * inverse), 0.0)
        done.append(work[:8])
        work = work[8:] if start + 8 < rank else None
    full = jnp.concatenate(done, axis=0)
    pivots = jnp.sum(jnp.where(lanes == rows, full, 0.0), axis=1, keepdims=True)
    full = full / jnp.sqrt(pivots)
    upper = jnp.where(lanes >= rows, full, 0.0)[:, :rank]
    return upper, full[:, rank:]


def kernel(
    nl, nb, scale,
    cols, count, fcols, near_hbm, probes_hbm, mix, far_hbm,
    coup, root,
    pv, nv, fv, ywin, part, pair, sums, scat, gbuf, gleaf, ubuf, ball,
    pin, win, h_s, h_r, f_s, f_r, p_s, p_r, r_s, r_r, g_s, g_r, gl_s, gl_r,
    u_s, u_r, bm_s, bm_r, bz_s, bz_r, bl_s, bl_r, bx_s, bx_r,
):
    leaf = lax.axis_index("leaf")
    blk = lax.axis_index("blk")
    R = pv.shape[0]
    half = R // 2
    nz = nb // 2
    groups = nb // R
    size = pv.shape[1]
    rank = mix.shape[1]
    near_dev = nv.shape[1]
    far_dev = fv.shape[1]
    core = blk % 2
    own = blk % R
    z = own // 2
    base = blk - own
    mate = blk + 1 - 2 * core
    pending = []

    def remote(src, dst, send, recv, to_leaf, to_blk):
        return pltpu.make_async_remote_copy(
            src_ref=src, dst_ref=dst, send_sem=send, recv_sem=recv,
            device_id=(to_leaf, to_blk), device_id_type=MESH,
        )

    loads = []
    for k in range(half):
        loads.append(pltpu.make_async_copy(probes_hbm.at[2 * k + core], pv.at[2 * k + core], pin.at[k]))
    for k in range(half):
        i = 2 * k + 1 - core
        loads.append(pltpu.make_async_copy(probes_hbm.at[i], pv.at[i], pin.at[half + k]))
    near_load = pltpu.make_async_copy(near_hbm, nv, win.at[0])
    far_load = pltpu.make_async_copy(far_hbm, fv, win.at[1])
    for load in loads:
        load.start()
    near_load.start()
    far_load.start()

    barrier = pltpu.get_barrier_semaphore()
    for d in range(1, nl):
        pl.semaphore_signal(barrier, inc=1, device_id=((leaf + d) % nl, blk), device_id_type=MESH)
    for d in range(1, nb):
        pl.semaphore_signal(barrier, inc=1, device_id=(leaf, (blk + d) % nb), device_id_type=MESH)

    terms = split_terms(mix[...])

    def mixed(i):
        product = jnp.dot(pv[i], terms, preferred_element_type=f32)
        ywin[R + i] = split_terms(product[:, :rank] + product[:, rank:])

    def up_copy(k):
        i = 2 * k + core
        return remote(ywin.at[R + i], ywin.at[i], h_s.at[k], h_r.at[k], (leaf + 1) % nl, blk)

    def down_copy(k):
        i = 2 * k + core
        return remote(
            ywin.at[R + i], ywin.at[2 * R + i], h_s.at[half + k], h_r.at[half + k], (leaf + nl - 1) % nl, blk
        )

    def share(side, k, parity):
        i = 2 * R * side + 2 * k + parity
        s = side * half + k
        return remote(ywin.at[i], ywin.at[i], f_s.at[s], f_r.at[s], leaf, mate)

    has_up = leaf < nl - 1
    has_down = leaf > 0
    for k in range(half):
        loads[k].wait()
        mixed(2 * k + core)
        if k == 0:
            pl.semaphore_wait(barrier, nl - 1 + nb - 1)

        @pl.when(has_up)
        def _():
            up_copy(k).start()

        @pl.when(has_down)
        def _():
            down_copy(k).start()

    for k in range(half):
        loads[half + k].wait()
        mixed(2 * k + 1 - core)

    @pl.when(jnp.logical_not(has_down))
    def _():
        ywin[0:R] = jnp.zeros((R,) + ywin.shape[1:], bf16)

    @pl.when(jnp.logical_not(has_up))
    def _():
        ywin[2 * R : 3 * R] = jnp.zeros((R,) + ywin.shape[1:], bf16)

    for k in range(half):

        @pl.when(has_down)
        def _():
            up_copy(k).wait_recv()
            share(0, k, core).start()

        @pl.when(has_up)
        def _():
            down_copy(k).wait_recv()
            share(1, k, core).start()

    for k in range(half):

        @pl.when(has_down)
        def _():
            share(0, k, 1 - core).wait_recv()

        @pl.when(has_up)
        def _():
            share(1, k, 1 - core).wait_recv()

    near_load.wait()

    def compressed(r):
        total = jnp.zeros((size, rank), f32)
        for s in range(near_dev):
            column = jnp.clip(cols[r, s] - (leaf - 1) * R, 0, 3 * R - 1)
            product = jnp.dot(nv[r, s], ywin[column], preferred_element_type=f32)
            live = blk * near_dev + s < count[r]
            total += jnp.where(live, product[:, :rank] + product[:, rank:], 0.0)
        return jnp.concatenate([total[: size // 2], total[size // 2 :]], axis=1)

    for k in range(half):
        part[k] = compressed(2 * k + 1 - core)
        copy = remote(part.at[k], pair.at[k], p_s.at[k], p_r.at[k], leaf, mate)
        copy.start()
        pending.append(copy)

    slot = blk // 2
    for k in range(half):
        mine = compressed(2 * k + core)
        pending[k].wait_recv()
        sums[k] = mine + pair[k]
        for g in range(groups):
            target = g * R + 2 * k + core

            @pl.when(target != blk)
            def _():
                remote(sums.at[k], scat.at[slot], r_s.at[k, g], r_r.at[slot], leaf, target).start()

            @pl.when(target == blk)
            def _():
                scat[slot] = sums[k]

    for d in range(1, nz):
        s = (slot + d) % nz
        remote(sums.at[0], scat.at[s], r_s.at[0, 0], r_r.at[s], leaf, mate).wait_recv()
    x = scat[0]
    for s in range(1, nz):
        x = x + scat[s]

    product = lax.dot_general(x, x, (((0,), (0,)), ((), ())), precision=highest, preferred_element_type=f32)
    gram = product[:rank, :rank] + product[rank:, rank:]
    gbuf[own] = gram
    for d in range(1, R):
        j = (own + d) % R
        copy = remote(gbuf.at[own], gbuf.at[own], g_s.at[d], g_r.at[own], leaf, base + j)
        copy.start()
        pending.append(copy)

    upper, inverse = factor(gram)
    zero = jnp.zeros((rank, rank), f32)
    twice = jnp.concatenate(
        [jnp.concatenate([inverse, zero], axis=1), jnp.concatenate([zero, inverse], axis=1)], axis=0
    )
    basis = lax.dot_general(x, twice, (((1,), (1,)), ((), ())), precision=highest, preferred_element_type=f32)

    def place(q_leaf, parity, q_z):
        return (q_leaf * 2 + parity) * half + q_z

    def spread(q_z):
        at = place(leaf, core, q_z)
        copies = [remote(ball.at[at], ball.at[at], bm_s.at[q_z], bm_r.at[q_z], leaf, mate)]
        for d in range(1, nl):
            copies.append(
                remote(
                    ball.at[at], ball.at[at], bl_s.at[d, q_z], bl_r.at[leaf, q_z], (leaf + d) % nl, blk
                )
            )
        for copy in copies:
            copy.start()
            pending.append(copy)

    at = place(leaf, core, z)
    ball[at] = basis.astype(bf16)
    for d in range(1, half):
        to = (z + d) % half
        copy = remote(ball.at[at], ball.at[at], bz_s.at[d], bz_r.at[z], leaf, base + 2 * to + core)
        copy.start()
        pending.append(copy)
    spread(z)
    ubuf[own] = upper
    for d in range(1, R):
        j = (own + d) % R
        copy = remote(ubuf.at[own], ubuf.at[own], u_s.at[d], u_r.at[own], leaf, base + j)
        copy.start()
        pending.append(copy)

    for d in range(1, R):
        j = (own + d) % R
        remote(gbuf.at[j], gbuf.at[j], g_s.at[d], g_r.at[j], leaf, mate).wait_recv()
    gram = gbuf[0]
    for j in range(1, R):
        gram = gram + gbuf[j]
    gleaf[leaf] = gram
    for d in range(1, nl):
        copy = remote(gleaf.at[leaf], gleaf.at[leaf], gl_s.at[d], gl_r.at[leaf], (leaf + d) % nl, blk)
        copy.start()
        pending.append(copy)

    for d in range(1, half):
        other = (z + d) % half
        at = place(leaf, core, other)
        remote(ball.at[at], ball.at[at], bz_s.at[d], bz_r.at[other], leaf, mate).wait_recv()
        spread(other)

    for d in range(1, nl):
        s = (leaf + d) % nl
        remote(gleaf.at[s], gleaf.at[s], gl_s.at[d], gl_r.at[s], s, blk).wait_recv()
    gram = gleaf[0]
    for s in range(1, nl):
        gram = gram + gleaf[s]
    _, root_inverse = factor(gram)

    for d in range(1, nl):
        s = (leaf + nl - d) % nl
        for k in range(half):
            at = place(s, core, k)
            remote(ball.at[at], ball.at[at], bl_s.at[d, k], bl_r.at[s, k], s, blk).wait_recv()
        span = pl.ds(place(s, core, 0), half)
        copy = remote(ball.at[span], ball.at[span], bx_s.at[d], bx_r.at[s], leaf, mate)
        copy.start()
        pending.append(copy)

    for d in range(1, R):
        j = (own + d) % R
        remote(ubuf.at[j], ubuf.at[j], u_s.at[d], u_r.at[j], leaf, mate).wait_recv()
    for r in range(R):
        root[r] = scale * lax.dot_general(
            ubuf[r], root_inverse, (((1,), (1,)), ((), ())), precision=highest, preferred_element_type=f32
        )

    for k in range(half):
        at = place(leaf, 1 - core, k)
        remote(ball.at[at], ball.at[at], bm_s.at[k], bm_r.at[k], leaf, mate).wait_recv()
    for d in range(1, nl):
        s = (leaf + nl - d) % nl
        span = pl.ds(place(s, 1 - core, 0), half)
        remote(ball.at[span], ball.at[span], bx_s.at[d], bx_r.at[s], leaf, mate).wait_recv()
    far_load.wait()

    def unpacked(block):
        return jnp.concatenate([block[:, :rank], block[:, rank:]], axis=0)

    for r in range(R):
        left = unpacked(ball[place(leaf, r % 2, r // 2)])
        for s in range(far_dev):
            q = fcols[r, s]
            right = unpacked(ball[place(q // R, q % 2, (q % R) // 2)])
            image = jnp.dot(fv[r, s], right, preferred_element_type=f32)
            product = lax.dot_general(
                left, split_terms(image), (((0,), (0,)), ((), ())), preferred_element_type=f32
            )
            coup[r, s] = product[:, :rank] + product[:, rank:]

    for copy in pending:
        copy.wait_send()
    for k in range(half):

        @pl.when(has_up)
        def _():
            up_copy(k).wait_send()
            share(1, k, core).wait_send()

        @pl.when(has_down)
        def _():
            down_copy(k).wait_send()
            share(0, k, core).wait_send()

        for g in range(groups):
            target = g * R + 2 * k + core

            @pl.when(target != blk)
            def _():
                remote(sums.at[k], scat.at[slot], r_s.at[k, g], r_r.at[slot], leaf, target).wait_send()


def shards(near_tiles, near_cols, near_count, probes, mixing, far_tiles, far_cols):
    nl, nb = lax.axis_size("leaf"), lax.axis_size("blk")
    R, size, width = probes.shape
    rank = mixing.shape[1]
    half, nz, groups = R // 2, nb // 2, nb // R
    assert R % 2 == 0 and nb % R == 0 and REACH <= R and nl > 1
    dma = pltpu.SemaphoreType.DMA
    packed = (size // 2, 2 * rank)
    vmem = pl.BlockSpec(memory_space=pltpu.VMEM)
    smem = pl.BlockSpec(memory_space=pltpu.SMEM)
    hbm = pl.BlockSpec(memory_space=pl.ANY)
    scale = math.sqrt(nl * R * rank)
    return pl.pallas_call(
        functools.partial(kernel, nl, nb, scale),
        out_shape=(
            jax.ShapeDtypeStruct((R, far_tiles.shape[1], rank, rank), f32),
            jax.ShapeDtypeStruct((R, rank, rank), f32),
        ),
        in_specs=[smem, smem, smem, hbm, hbm, vmem, hbm],
        out_specs=(vmem, vmem),
        scratch_shapes=[
            pltpu.VMEM(probes.shape, bf16),
            pltpu.VMEM(near_tiles.shape, bf16),
            pltpu.VMEM(far_tiles.shape, bf16),
            pltpu.VMEM((3 * R, size, 2 * rank), bf16),
            pltpu.VMEM((half,) + packed, f32),
            pltpu.VMEM((half,) + packed, f32),
            pltpu.VMEM((half,) + packed, f32),
            pltpu.VMEM((nz,) + packed, f32),
            pltpu.VMEM((R, rank, rank), f32),
            pltpu.VMEM((nl, rank, rank), f32),
            pltpu.VMEM((R, rank, rank), f32),
            pltpu.VMEM((nl * R,) + packed, bf16),
            dma((R,)), dma((2,)),
            dma((R,)), dma((R,)), dma((R,)), dma((R,)),
            dma((half,)), dma((half,)),
            dma((half, groups)), dma((nz,)),
            dma((R,)), dma((R,)), dma((nl,)), dma((nl,)),
            dma((R,)), dma((R,)), dma((half,)), dma((half,)),
            dma((half,)), dma((half,)),
            dma((nl, half)), dma((nl, half)), dma((nl,)), dma((nl,)),
        ],
        compiler_params=pltpu.CompilerParams(
            collective_id=0, has_side_effects=True, vmem_limit_bytes=48 * 1024 * 1024
        ),
        name="nested_basis",
    )(near_cols, near_count, far_cols, near_tiles, probes, mixing, far_tiles)


def solution(mesh):
    in_specs = (
        P("leaf", "blk", None, None),
        P("leaf", "blk"),
        P("leaf"),
        P("leaf", None, None),
        P(),
        P("leaf", "blk", None, None),
        P("leaf", "blk"),
    )
    out_specs = (P("leaf", "blk", None, None), P("leaf", None, None))
    return jax.shard_map(shards, mesh=mesh, in_specs=in_specs, out_specs=out_specs, check_vma=False)
```

```python
import functools
import math

import jax
import jax.numpy as jnp
from jax import lax
from jax.experimental import pallas as pl
from jax.experimental.pallas import tpu as pltpu
from jax.sharding import PartitionSpec as P

REACH = 8
MESH = pl.DeviceIdType.MESH
highest = lax.Precision.HIGHEST
f32 = jnp.float32
bf16 = jnp.bfloat16


def split_terms(value):
    high = value.astype(bf16)
    low = (value - high.astype(f32)).astype(bf16)
    return jnp.concatenate([high, low], axis=1)


def factor(gram):
    rank = gram.shape[0]
    rows = lax.broadcasted_iota(jnp.int32, (rank, 2 * rank), 0)
    lanes = lax.broadcasted_iota(jnp.int32, (rank, 2 * rank), 1)
    unit = jnp.where(lanes - rank == rows, 1.0, 0.0).astype(f32)
    work = jnp.where(lanes < rank, jnp.concatenate([gram, gram], axis=1), unit)
    done = []
    for start in range(0, rank, 8):
        index = lax.broadcasted_iota(jnp.int32, work.shape, 0)
        for step in range(8):
            j = start + step
            row = work[step : step + 1, :]
            inverse = 1.0 / work[step : step + 1, j : j + 1]
            column = work[:, j : j + 1]
            work = work - jnp.where(index > step, column * (row * inverse), 0.0)
        done.append(work[:8])
        work = work[8:] if start + 8 < rank else None
    full = jnp.concatenate(done, axis=0)
    pivots = jnp.sum(jnp.where(lanes == rows, full, 0.0), axis=1, keepdims=True)
    full = full / jnp.sqrt(pivots)
    upper = jnp.where(lanes >= rows, full, 0.0)[:, :rank]
    return upper, full[:, rank:]


def kernel(
    nl, nb, scale,
    cols_hbm, count_hbm, fcols_hbm, near_hbm, probes_hbm, mix_hbm, far_hbm,
    coup, root,
    cols, count, fcols, mix, pv, nv, fv, ywin, part, pair, sums, scat, gbuf, gleaf, ubuf, ball,
    pin, win, h_s, h_r, q_s, q_r, f_s, f_r, p_s, p_r, r_s, r_r, g_s, g_r, gl_s, gl_r,
    u_s, u_r, bm_s, bm_r, bz_s, bz_r, bl_s, bl_r, bx_s, bx_r,
):
    leaf = lax.axis_index("leaf")
    blk = lax.axis_index("blk")
    R = pv.shape[0]
    half = R // 2
    nz = nb // 2
    groups = nb // R
    size = pv.shape[1]
    rank = mix.shape[0]
    near_dev = nv.shape[1]
    far_dev = fv.shape[1]
    core = blk % 2
    own = blk % R
    z = own // 2
    base = blk - own
    mate = blk + 1 - 2 * core
    turn = (blk // 2) % 2
    beside = blk + 2 - 4 * turn
    quarter = half // 2
    pending = []

    def remote(src, dst, send, recv, to_leaf, to_blk):
        return pltpu.make_async_remote_copy(
            src_ref=src, dst_ref=dst, send_sem=send, recv_sem=recv,
            device_id=(to_leaf, to_blk), device_id_type=MESH,
        )

    order = [2 * (2 * m + turn) + core for m in range(quarter)]
    order += [2 * (2 * m + 1 - turn) + core for m in range(quarter)]
    order += [2 * k + 1 - core for k in range(half)]
    mix_load = pltpu.make_async_copy(mix_hbm, mix, win.at[2])
    mix_load.start()
    loads = [pltpu.make_async_copy(probes_hbm.at[i], pv.at[i], pin.at[k]) for k, i in enumerate(order)]
    near_load = pltpu.make_async_copy(near_hbm, nv, win.at[0])
    far_load = pltpu.make_async_copy(far_hbm, fv, win.at[1])
    small_loads = [
        pltpu.make_async_copy(cols_hbm, cols, win.at[3]),
        pltpu.make_async_copy(count_hbm, count, win.at[4]),
        pltpu.make_async_copy(fcols_hbm, fcols, win.at[5]),
    ]
    for load in loads + small_loads + [near_load, far_load]:
        load.start()

    barrier = pltpu.get_barrier_semaphore()
    for d in range(1, nl):
        pl.semaphore_signal(barrier, inc=1, device_id=((leaf + d) % nl, blk), device_id_type=MESH)
    for d in range(1, nb):
        pl.semaphore_signal(barrier, inc=1, device_id=(leaf, (blk + d) % nb), device_id_type=MESH)

    mix_load.wait()
    high = mix[...].astype(bf16).astype(f32)
    terms = jnp.concatenate([high, mix[...] - high], axis=0).T.astype(bf16)

    def mixed(i):
        product = jnp.dot(pv[i], terms, preferred_element_type=f32)
        ywin[R + i] = split_terms(product[:, :rank] + product[:, rank:])

    def over_leaf(side, m):
        i = 2 * (2 * m + turn) + core
        at = side * quarter + m
        to = (leaf + 1) % nl if side == 0 else (leaf + nl - 1) % nl
        return remote(ywin.at[R + i], ywin.at[2 * R * side + i], h_s.at[at], h_r.at[at], to, blk)

    def over_z(side, m, whose):
        i = 2 * R * side + 2 * (2 * m + whose) + core
        at = side * quarter + m
        return remote(ywin.at[i], ywin.at[i], q_s.at[at], q_r.at[at], leaf, beside)

    def share(side, k, parity):
        i = 2 * R * side + 2 * k + parity
        at = side * half + k
        return remote(ywin.at[i], ywin.at[i], f_s.at[at], f_r.at[at], leaf, mate)

    has_up = leaf < nl - 1
    has_down = leaf > 0
    sends = (has_up, has_down)
    gets = (has_down, has_up)
    for m in range(quarter):
        loads[m].wait()
        mixed(order[m])
        if m == 0:
            pl.semaphore_wait(barrier, nl - 1 + nb - 1)
        for side in range(2):

            @pl.when(sends[side])
            def _():
                over_leaf(side, m).start()

    for k in range(quarter, R):
        loads[k].wait()
        mixed(order[k])

    for side in range(2):

        @pl.when(jnp.logical_not(gets[side]))
        def _():
            ywin[2 * R * side : 2 * R * side + R] = jnp.zeros((R,) + ywin.shape[1:], bf16)

    for m in range(quarter):
        for side in range(2):

            @pl.when(gets[side])
            def _():
                over_leaf(side, m).wait_recv()
                over_z(side, m, turn).start()
                share(side, 2 * m + turn, core).start()

    for m in range(quarter):
        for side in range(2):

            @pl.when(gets[side])
            def _():
                over_z(side, m, 1 - turn).wait_recv()
                share(side, 2 * m + 1 - turn, core).start()

    for k in range(half):
        for side in range(2):

            @pl.when(gets[side])
            def _():
                share(side, k, 1 - core).wait_recv()

    for load in small_loads:
        load.wait()
    near_load.wait()

    def compressed(r):
        total = jnp.zeros((size, rank), f32)
        for s in range(near_dev):
            column = jnp.clip(cols[s, r] - (leaf - 1) * R, 0, 3 * R - 1)
            product = jnp.dot(nv[r, s], ywin[column], preferred_element_type=f32)
            live = blk * near_dev + s < count[r]
            total += jnp.where(live, product[:, :rank] + product[:, rank:], 0.0)
        return jnp.concatenate([total[: size // 2], total[size // 2 :]], axis=1)

    for k in range(half):
        part[k] = compressed(2 * k + 1 - core)
        copy = remote(part.at[k], pair.at[k], p_s.at[k], p_r.at[k], leaf, mate)
        copy.start()
        pending.append(copy)

    slot = blk // 2
    for k in range(half):
        mine = compressed(2 * k + core)
        pending[k].wait_recv()
        sums[k] = mine + pair[k]
        for g in range(groups):
            target = g * R + 2 * k + core

            @pl.when(target != blk)
            def _():
                remote(sums.at[k], scat.at[slot], r_s.at[k, g], r_r.at[slot], leaf, target).start()

            @pl.when(target == blk)
            def _():
                scat[slot] = sums[k]

    for d in range(1, nz):
        s = (slot + d) % nz
        remote(sums.at[0], scat.at[s], r_s.at[0, 0], r_r.at[s], leaf, mate).wait_recv()
    x = scat[0]
    for s in range(1, nz):
        x = x + scat[s]

    product = lax.dot_general(x, x, (((0,), (0,)), ((), ())), precision=highest, preferred_element_type=f32)
    gram = product[:rank, :rank] + product[rank:, rank:]
    gbuf[own] = gram
    for d in range(1, R):
        j = (own + d) % R
        copy = remote(gbuf.at[own], gbuf.at[own], g_s.at[d], g_r.at[own], leaf, base + j)
        copy.start()
        pending.append(copy)

    upper, inverse = factor(gram)
    zero = jnp.zeros((rank, rank), f32)
    twice = jnp.concatenate(
        [jnp.concatenate([inverse, zero], axis=1), jnp.concatenate([zero, inverse], axis=1)], axis=0
    )
    basis = lax.dot_general(x, twice, (((1,), (1,)), ((), ())), precision=highest, preferred_element_type=f32)

    def place(q_leaf, parity, q_z):
        return (q_leaf * 2 + parity) * half + q_z

    def spread(q_z):
        at = place(leaf, core, q_z)
        copies = [remote(ball.at[at], ball.at[at], bm_s.at[q_z], bm_r.at[q_z], leaf, mate)]
        for d in range(1, nl):
            copies.append(
                remote(
                    ball.at[at], ball.at[at], bl_s.at[d, q_z], bl_r.at[leaf, q_z], (leaf + d) % nl, blk
                )
            )
        for copy in copies:
            copy.start()
            pending.append(copy)

    at = place(leaf, core, z)
    ball[at] = basis.astype(bf16)
    for d in range(1, half):
        to = (z + d) % half
        copy = remote(ball.at[at], ball.at[at], bz_s.at[d], bz_r.at[z], leaf, base + 2 * to + core)
        copy.start()
        pending.append(copy)
    spread(z)
    ubuf[own] = upper
    for d in range(1, R):
        j = (own + d) % R
        copy = remote(ubuf.at[own], ubuf.at[own], u_s.at[d], u_r.at[own], leaf, base + j)
        copy.start()
        pending.append(copy)

    for d in range(1, R):
        j = (own + d) % R
        remote(gbuf.at[j], gbuf.at[j], g_s.at[d], g_r.at[j], leaf, mate).wait_recv()
    gram = gbuf[0]
    for j in range(1, R):
        gram = gram + gbuf[j]
    gleaf[leaf] = gram
    for d in range(1, nl):
        copy = remote(gleaf.at[leaf], gleaf.at[leaf], gl_s.at[d], gl_r.at[leaf], (leaf + d) % nl, blk)
        copy.start()
        pending.append(copy)

    for d in range(1, half):
        other = (z + d) % half
        at = place(leaf, core, other)
        remote(ball.at[at], ball.at[at], bz_s.at[d], bz_r.at[other], leaf, mate).wait_recv()
        spread(other)

    for d in range(1, nl):
        s = (leaf + d) % nl
        remote(gleaf.at[s], gleaf.at[s], gl_s.at[d], gl_r.at[s], s, blk).wait_recv()
    gram = gleaf[0]
    for s in range(1, nl):
        gram = gram + gleaf[s]
    _, root_inverse = factor(gram)

    for d in range(1, nl):
        s = (leaf + nl - d) % nl
        for k in range(half):
            at = place(s, core, k)
            remote(ball.at[at], ball.at[at], bl_s.at[d, k], bl_r.at[s, k], s, blk).wait_recv()
        span = pl.ds(place(s, core, 0), half)
        copy = remote(ball.at[span], ball.at[span], bx_s.at[d], bx_r.at[s], leaf, mate)
        copy.start()
        pending.append(copy)

    for d in range(1, R):
        j = (own + d) % R
        remote(ubuf.at[j], ubuf.at[j], u_s.at[d], u_r.at[j], leaf, mate).wait_recv()
    for r in range(R):
        root[r] = scale * lax.dot_general(
            ubuf[r], root_inverse, (((1,), (1,)), ((), ())), precision=highest, preferred_element_type=f32
        )

    for k in range(half):
        at = place(leaf, 1 - core, k)
        remote(ball.at[at], ball.at[at], bm_s.at[k], bm_r.at[k], leaf, mate).wait_recv()
    for d in range(1, nl):
        s = (leaf + nl - d) % nl
        span = pl.ds(place(s, 1 - core, 0), half)
        remote(ball.at[span], ball.at[span], bx_s.at[d], bx_r.at[s], leaf, mate).wait_recv()
    far_load.wait()

    def unpacked(block):
        return jnp.concatenate([block[:, :rank], block[:, rank:]], axis=0)

    for r in range(R):
        left = unpacked(ball[place(leaf, r % 2, r // 2)])
        for s in range(far_dev):
            q = fcols[s, r]
            right = unpacked(ball[place(q // R, q % 2, (q % R) // 2)])
            image = jnp.dot(fv[r, s], right, preferred_element_type=f32)
            product = lax.dot_general(
                left, split_terms(image), (((0,), (0,)), ((), ())), preferred_element_type=f32
            )
            coup[r, s] = product[:, :rank] + product[:, rank:]

    for copy in pending:
        copy.wait_send()
    for side in range(2):
        for m in range(quarter):

            @pl.when(sends[side])
            def _():
                over_leaf(side, m).wait_send()

            @pl.when(gets[side])
            def _():
                over_z(side, m, turn).wait_send()

        for k in range(half):

            @pl.when(gets[side])
            def _():
                share(side, k, core).wait_send()

    for k in range(half):
        for g in range(groups):
            target = g * R + 2 * k + core

            @pl.when(target != blk)
            def _():
                remote(sums.at[k], scat.at[slot], r_s.at[k, g], r_r.at[slot], leaf, target).wait_send()


def shards(near_tiles, near_cols, near_count, probes, mixing, far_tiles, far_cols):
    nl, nb = lax.axis_size("leaf"), lax.axis_size("blk")
    R, size, width = probes.shape
    rank = mixing.shape[1]
    half, nz, groups = R // 2, nb // 2, nb // R
    assert R % 4 == 0 and nb % R == 0 and REACH <= R and nl > 1
    dma = pltpu.SemaphoreType.DMA
    packed = (size // 2, 2 * rank)
    vmem = pl.BlockSpec(memory_space=pltpu.VMEM)
    hbm = pl.BlockSpec(memory_space=pl.ANY)
    scale = math.sqrt(nl * R * rank)
    return pl.pallas_call(
        functools.partial(kernel, nl, nb, scale),
        out_shape=(
            jax.ShapeDtypeStruct((R, far_tiles.shape[1], rank, rank), f32),
            jax.ShapeDtypeStruct((R, rank, rank), f32),
        ),
        in_specs=[hbm] * 7,
        out_specs=(vmem, vmem),
        scratch_shapes=[
            pltpu.SMEM(near_cols.shape[::-1], jnp.int32),
            pltpu.SMEM(near_count.shape, jnp.int32),
            pltpu.SMEM(far_cols.shape[::-1], jnp.int32),
            pltpu.VMEM(mixing.shape[::-1], f32),
            pltpu.VMEM(probes.shape, bf16),
            pltpu.VMEM(near_tiles.shape, bf16),
            pltpu.VMEM(far_tiles.shape, bf16),
            pltpu.VMEM((3 * R, size, 2 * rank), bf16),
            pltpu.VMEM((half,) + packed, f32),
            pltpu.VMEM((half,) + packed, f32),
            pltpu.VMEM((half,) + packed, f32),
            pltpu.VMEM((nz,) + packed, f32),
            pltpu.VMEM((R, rank, rank), f32),
            pltpu.VMEM((nl, rank, rank), f32),
            pltpu.VMEM((R, rank, rank), f32),
            pltpu.VMEM((nl * R,) + packed, bf16),
            dma((R,)), dma((6,)),
            dma((half,)), dma((half,)), dma((half,)), dma((half,)), dma((R,)), dma((R,)),
            dma((half,)), dma((half,)),
            dma((half, groups)), dma((nz,)),
            dma((R,)), dma((R,)), dma((nl,)), dma((nl,)),
            dma((R,)), dma((R,)), dma((half,)), dma((half,)),
            dma((half,)), dma((half,)),
            dma((nl, half)), dma((nl, half)), dma((nl,)), dma((nl,)),
        ],
        compiler_params=pltpu.CompilerParams(
            collective_id=0, has_side_effects=True, vmem_limit_bytes=60 * 1024 * 1024
        ),
        name="nested_basis",
    )(near_cols.T, near_count, far_cols.T, near_tiles, probes, mixing.T, far_tiles)


def solution(mesh):
    in_specs = (
        P("leaf", "blk", None, None),
        P("leaf", "blk"),
        P("leaf"),
        P("leaf", None, None),
        P(),
        P("leaf", "blk", None, None),
        P("leaf", "blk"),
    )
    out_specs = (P("leaf", "blk", None, None), P("leaf", None, None))
    return jax.shard_map(shards, mesh=mesh, in_specs=in_specs, out_specs=out_specs, check_vma=False)
```

```python
import functools
import math

import jax
import jax.numpy as jnp
from jax import lax
from jax.experimental import pallas as pl
from jax.experimental.pallas import tpu as pltpu
from jax.sharding import PartitionSpec as P

REACH = 8
MESH = pl.DeviceIdType.MESH
highest = lax.Precision.HIGHEST
f32 = jnp.float32
bf16 = jnp.bfloat16


def split_terms(value):
    high = value.astype(bf16)
    low = (value - high.astype(f32)).astype(bf16)
    return jnp.concatenate([high, low], axis=1)


def factor(gram):
    rank = gram.shape[0]
    rows = lax.broadcasted_iota(jnp.int32, (rank, 2 * rank), 0)
    lanes = lax.broadcasted_iota(jnp.int32, (rank, 2 * rank), 1)
    unit = jnp.where(lanes - rank == rows, 1.0, 0.0).astype(f32)
    work = jnp.where(lanes < rank, jnp.concatenate([gram, gram], axis=1), unit)
    done = []
    for start in range(0, rank, 8):
        index = lax.broadcasted_iota(jnp.int32, work.shape, 0)
        for step in range(0, 8, 2):
            j = start + step
            row_a = work[step : step + 1, :]
            row_b = work[step + 1 : step + 2, :]
            column_a = work[:, j : j + 1]
            column_b = work[:, j + 1 : j + 2]
            inverse_a = 1.0 / work[step : step + 1, j : j + 1]
            cross = work[step : step + 1, j + 1 : j + 2]
            ratio = cross * inverse_a
            inverse_b = 1.0 / (work[step + 1 : step + 2, j + 1 : j + 2] - cross * ratio)
            row_b = row_b - ratio * row_a
            column_b = column_b - ratio * column_a
            first = jnp.where(index > step, column_a * (row_a * inverse_a), 0.0)
            second = jnp.where(index > step + 1, column_b * (row_b * inverse_b), 0.0)
            work = work - first - second
        done.append(work[:8])
        work = work[8:] if start + 8 < rank else None
    full = jnp.concatenate(done, axis=0)
    pivots = jnp.sum(jnp.where(lanes == rows, full, 0.0), axis=1, keepdims=True)
    full = full / jnp.sqrt(pivots)
    upper = jnp.where(lanes >= rows, full, 0.0)[:, :rank]
    return upper, full[:, rank:]


def kernel(
    nl, nb, scale,
    cols_hbm, count_hbm, fcols_hbm, near_hbm, probes_hbm, mix_hbm, far_hbm,
    coup, root,
    cols, count, fcols, mix, pv, nv, fv, ywin, part, pair, sums, scat, gbuf, gleaf, ubuf, ball, front,
    pin, win, h_s, h_r, q_s, q_r, f_s, f_r, p_s, p_r, r_s, r_r, g_s, g_r, gl_s, gl_r,
    u_s, u_r, bm_s, bm_r, bz_s, bz_r, bl_s, bl_r, bx_s, bx_r,
):
    leaf = lax.axis_index("leaf")
    blk = lax.axis_index("blk")
    R = pv.shape[0]
    half = R // 2
    nz = nb // 2
    groups = nb // R
    size = pv.shape[1]
    rank = mix.shape[0]
    near_dev = nv.shape[1]
    far_dev = fv.shape[1]
    core = blk % 2
    own = blk % R
    z = own // 2
    base = blk - own
    mate = blk + 1 - 2 * core
    turn = (blk // 2) % 2
    beside = blk + 2 - 4 * turn
    quarter = half // 2
    pending = []

    def remote(src, dst, send, recv, to_leaf, to_blk):
        return pltpu.make_async_remote_copy(
            src_ref=src, dst_ref=dst, send_sem=send, recv_sem=recv,
            device_id=(to_leaf, to_blk), device_id_type=MESH,
        )

    order = [2 * (2 * m + turn) + core for m in range(quarter)]
    order += [2 * (2 * m + 1 - turn) + core for m in range(quarter)]
    order += [2 * k + 1 - core for k in range(half)]
    mix_load = pltpu.make_async_copy(mix_hbm, mix, win.at[2])
    mix_load.start()
    loads = [pltpu.make_async_copy(probes_hbm.at[i], pv.at[i], pin.at[k]) for k, i in enumerate(order)]
    near_load = pltpu.make_async_copy(near_hbm, nv, win.at[0])
    far_load = pltpu.make_async_copy(far_hbm, fv, win.at[1])
    small_loads = [
        pltpu.make_async_copy(cols_hbm, cols, win.at[3]),
        pltpu.make_async_copy(count_hbm, count, win.at[4]),
        pltpu.make_async_copy(fcols_hbm, fcols, win.at[5]),
    ]
    for load in loads + small_loads + [near_load, far_load]:
        load.start()

    barrier = pltpu.get_barrier_semaphore()
    for d in range(1, nl):
        pl.semaphore_signal(barrier, inc=1, device_id=((leaf + d) % nl, blk), device_id_type=MESH)
    for d in range(1, nb):
        pl.semaphore_signal(barrier, inc=1, device_id=(leaf, (blk + d) % nb), device_id_type=MESH)

    mix_load.wait()
    high = mix[...].astype(bf16).astype(f32)
    terms = jnp.concatenate([high, mix[...] - high], axis=0).T.astype(bf16)

    def mixed(i):
        product = jnp.dot(pv[i], terms, preferred_element_type=f32)
        ywin[R + i] = split_terms(product[:, :rank] + product[:, rank:])

    def over_leaf(side, m):
        i = 2 * (2 * m + turn) + core
        at = side * quarter + m
        to = (leaf + 1) % nl if side == 0 else (leaf + nl - 1) % nl
        return remote(ywin.at[R + i], ywin.at[2 * R * side + i], h_s.at[at], h_r.at[at], to, blk)

    def over_z(side, m, whose):
        i = 2 * R * side + 2 * (2 * m + whose) + core
        at = side * quarter + m
        return remote(ywin.at[i], ywin.at[i], q_s.at[at], q_r.at[at], leaf, beside)

    def share(side, k, parity):
        i = 2 * R * side + 2 * k + parity
        at = side * half + k
        return remote(ywin.at[i], ywin.at[i], f_s.at[at], f_r.at[at], leaf, mate)

    has_up = leaf < nl - 1
    has_down = leaf > 0
    sends = (has_up, has_down)
    gets = (has_down, has_up)
    for m in range(quarter):
        loads[m].wait()
        mixed(order[m])
        if m == 0:
            pl.semaphore_wait(barrier, nl - 1 + nb - 1)
        for side in range(2):

            @pl.when(sends[side])
            def _():
                over_leaf(side, m).start()

    for k in range(quarter, R):
        loads[k].wait()
        mixed(order[k])

    for side in range(2):

        @pl.when(jnp.logical_not(gets[side]))
        def _():
            ywin[2 * R * side : 2 * R * side + R] = jnp.zeros((R,) + ywin.shape[1:], bf16)

    for m in range(quarter):
        for side in range(2):

            @pl.when(gets[side])
            def _():
                over_leaf(side, m).wait_recv()
                over_z(side, m, turn).start()
                share(side, 2 * m + turn, core).start()

    for m in range(quarter):
        for side in range(2):

            @pl.when(gets[side])
            def _():
                over_z(side, m, 1 - turn).wait_recv()
                share(side, 2 * m + 1 - turn, core).start()

    for k in range(half):
        for side in range(2):

            @pl.when(gets[side])
            def _():
                share(side, k, 1 - core).wait_recv()

    for load in small_loads:
        load.wait()
    near_load.wait()

    def compressed(r):
        total = jnp.zeros((size, rank), f32)
        for s in range(near_dev):
            column = jnp.clip(cols[s, r] - (leaf - 1) * R, 0, 3 * R - 1)
            product = jnp.dot(nv[r, s], ywin[column], preferred_element_type=f32)
            live = blk * near_dev + s < count[r]
            total += jnp.where(live, product[:, :rank] + product[:, rank:], 0.0)
        return jnp.concatenate([total[: size // 2], total[size // 2 :]], axis=1)

    for k in range(half):
        part[k] = compressed(2 * k + 1 - core)
        copy = remote(part.at[k], pair.at[k], p_s.at[k], p_r.at[k], leaf, mate)
        copy.start()
        pending.append(copy)

    slot = blk // 2
    for k in range(half):
        mine = compressed(2 * k + core)
        pending[k].wait_recv()
        sums[k] = mine + pair[k]
        for g in range(groups):
            target = g * R + 2 * k + core

            @pl.when(target != blk)
            def _():
                remote(sums.at[k], scat.at[slot], r_s.at[k, g], r_r.at[slot], leaf, target).start()

            @pl.when(target == blk)
            def _():
                scat[slot] = sums[k]

    for d in range(1, nz):
        s = (slot + d) % nz
        remote(sums.at[0], scat.at[s], r_s.at[0, 0], r_r.at[s], leaf, mate).wait_recv()
    x = scat[0]
    for s in range(1, nz):
        x = x + scat[s]

    product = lax.dot_general(x, x, (((0,), (0,)), ((), ())), precision=highest, preferred_element_type=f32)
    gram = product[:rank, :rank] + product[rank:, rank:]
    gbuf[own] = gram
    for d in range(1, R):
        j = (own + d) % R
        copy = remote(gbuf.at[own], gbuf.at[own], g_s.at[d], g_r.at[own], leaf, base + j)
        copy.start()
        pending.append(copy)

    upper, inverse = factor(gram)
    zero = jnp.zeros((rank, rank), f32)
    twice = jnp.concatenate(
        [jnp.concatenate([inverse, zero], axis=1), jnp.concatenate([zero, inverse], axis=1)], axis=0
    )
    basis = lax.dot_general(x, twice, (((1,), (1,)), ((), ())), precision=highest, preferred_element_type=f32)

    def place(q_leaf, parity, q_z):
        return (q_leaf * 2 + parity) * half + q_z

    def spread(q_z):
        at = place(leaf, core, q_z)
        copies = [remote(ball.at[at], ball.at[at], bm_s.at[q_z], bm_r.at[q_z], leaf, mate)]
        for d in range(1, nl):
            copies.append(
                remote(
                    ball.at[at], ball.at[at], bl_s.at[d, q_z], bl_r.at[leaf, q_z], (leaf + d) % nl, blk
                )
            )
        for copy in copies:
            copy.start()
            pending.append(copy)

    at = place(leaf, core, z)
    ball[at] = basis.astype(bf16)
    for d in range(1, half):
        to = (z + d) % half
        copy = remote(ball.at[at], ball.at[at], bz_s.at[d], bz_r.at[z], leaf, base + 2 * to + core)
        copy.start()
        pending.append(copy)
    spread(z)
    ubuf[own] = upper
    for d in range(1, R):
        j = (own + d) % R
        copy = remote(ubuf.at[own], ubuf.at[own], u_s.at[d], u_r.at[own], leaf, base + j)
        copy.start()
        pending.append(copy)

    for d in range(1, R):
        j = (own + d) % R
        remote(gbuf.at[j], gbuf.at[j], g_s.at[d], g_r.at[j], leaf, mate).wait_recv()
    gram = gbuf[0]
    for j in range(1, R):
        gram = gram + gbuf[j]
    gleaf[leaf] = gram
    for d in range(1, nl):
        copy = remote(gleaf.at[leaf], gleaf.at[leaf], gl_s.at[d], gl_r.at[leaf], (leaf + d) % nl, blk)
        copy.start()
        pending.append(copy)

    for d in range(1, half):
        other = (z + d) % half
        at = place(leaf, core, other)
        remote(ball.at[at], ball.at[at], bz_s.at[d], bz_r.at[other], leaf, mate).wait_recv()
        spread(other)

    for k in range(half):
        at = place(leaf, 1 - core, k)
        remote(ball.at[at], ball.at[at], bm_s.at[k], bm_r.at[k], leaf, mate).wait_recv()
    far_load.wait()
    middle = size // 2
    for r in range(R):
        block = ball[place(leaf, r % 2, r // 2)]
        left = jnp.concatenate([block[:, :rank], block[:, rank:]], axis=0)
        for s in range(far_dev):
            image = lax.dot_general(
                left, fv[r, s], (((0,), (0,)), ((), ())), preferred_element_type=f32
            )
            high = image.astype(bf16)
            low = (image - high.astype(f32)).astype(bf16)
            front[r, s] = jnp.concatenate(
                [high[:, :middle], low[:, :middle], high[:, middle:], low[:, middle:]], axis=0
            )

    def relay(d):
        s = (leaf + nl - d) % nl
        for k in range(half):
            at = place(s, core, k)
            remote(ball.at[at], ball.at[at], bl_s.at[d, k], bl_r.at[s, k], s, blk).wait_recv()
        span = pl.ds(place(s, core, 0), half)
        copy = remote(ball.at[span], ball.at[span], bx_s.at[d], bx_r.at[s], leaf, mate)
        copy.start()
        pending.append(copy)

    for d in range(1, nl):
        s = (leaf + d) % nl
        remote(gleaf.at[s], gleaf.at[s], gl_s.at[d], gl_r.at[s], s, blk).wait_recv()
    gram = gleaf[0]
    for s in range(1, nl):
        gram = gram + gleaf[s]
    _, root_inverse = factor(gram)

    for d in range(1, nl):
        relay(d)

    for d in range(1, R):
        j = (own + d) % R
        remote(ubuf.at[j], ubuf.at[j], u_s.at[d], u_r.at[j], leaf, mate).wait_recv()
    for r in range(R):
        root[r] = scale * lax.dot_general(
            ubuf[r], root_inverse, (((1,), (1,)), ((), ())), precision=highest, preferred_element_type=f32
        )

    for d in range(1, nl):
        s = (leaf + nl - d) % nl
        span = pl.ds(place(s, 1 - core, 0), half)
        remote(ball.at[span], ball.at[span], bx_s.at[d], bx_r.at[s], leaf, mate).wait_recv()

    for r in range(R):
        for s in range(far_dev):
            q = fcols[s, r]
            block = ball[place(q // R, q % 2, (q % R) // 2)]
            product = jnp.dot(front[r, s], block, preferred_element_type=f32)
            upper = product[:rank] + product[rank : 2 * rank]
            lower = product[2 * rank : 3 * rank] + product[3 * rank :]
            coup[r, s] = upper[:, :rank] + lower[:, rank:]

    for copy in pending:
        copy.wait_send()
    for side in range(2):
        for m in range(quarter):

            @pl.when(sends[side])
            def _():
                over_leaf(side, m).wait_send()

            @pl.when(gets[side])
            def _():
                over_z(side, m, turn).wait_send()

        for k in range(half):

            @pl.when(gets[side])
            def _():
                share(side, k, core).wait_send()

    for k in range(half):
        for g in range(groups):
            target = g * R + 2 * k + core

            @pl.when(target != blk)
            def _():
                remote(sums.at[k], scat.at[slot], r_s.at[k, g], r_r.at[slot], leaf, target).wait_send()


def shards(near_tiles, near_cols, near_count, probes, mixing, far_tiles, far_cols):
    nl, nb = lax.axis_size("leaf"), lax.axis_size("blk")
    R, size, width = probes.shape
    rank = mixing.shape[1]
    half, nz, groups = R // 2, nb // 2, nb // R
    assert R % 4 == 0 and nb % R == 0 and REACH <= R and nl > 1
    dma = pltpu.SemaphoreType.DMA
    packed = (size // 2, 2 * rank)
    vmem = pl.BlockSpec(memory_space=pltpu.VMEM)
    hbm = pl.BlockSpec(memory_space=pltpu.HBM)
    scale = math.sqrt(nl * R * rank)
    return pl.pallas_call(
        functools.partial(kernel, nl, nb, scale),
        out_shape=(
            jax.ShapeDtypeStruct((R, far_tiles.shape[1], rank, rank), f32),
            jax.ShapeDtypeStruct((R, rank, rank), f32),
        ),
        in_specs=[hbm] * 7,
        out_specs=(vmem, vmem),
        scratch_shapes=[
            pltpu.SMEM(near_cols.shape[::-1], jnp.int32),
            pltpu.SMEM(near_count.shape, jnp.int32),
            pltpu.SMEM(far_cols.shape[::-1], jnp.int32),
            pltpu.VMEM(mixing.shape[::-1], f32),
            pltpu.VMEM(probes.shape, bf16),
            pltpu.VMEM(near_tiles.shape, bf16),
            pltpu.VMEM(far_tiles.shape, bf16),
            pltpu.VMEM((3 * R, size, 2 * rank), bf16),
            pltpu.VMEM((half,) + packed, f32),
            pltpu.VMEM((half,) + packed, f32),
            pltpu.VMEM((half,) + packed, f32),
            pltpu.VMEM((nz,) + packed, f32),
            pltpu.VMEM((R, rank, rank), f32),
            pltpu.VMEM((nl, rank, rank), f32),
            pltpu.VMEM((R, rank, rank), f32),
            pltpu.VMEM((nl * R,) + packed, bf16),
            pltpu.VMEM((R, far_tiles.shape[1], 4 * rank, size // 2), bf16),
            dma((R,)), dma((6,)),
            dma((half,)), dma((half,)), dma((half,)), dma((half,)), dma((R,)), dma((R,)),
            dma((half,)), dma((half,)),
            dma((half, groups)), dma((nz,)),
            dma((R,)), dma((R,)), dma((nl,)), dma((nl,)),
            dma((R,)), dma((R,)), dma((half,)), dma((half,)),
            dma((half,)), dma((half,)),
            dma((nl, half)), dma((nl, half)), dma((nl,)), dma((nl,)),
        ],
        compiler_params=pltpu.CompilerParams(
            collective_id=0, has_side_effects=True, vmem_limit_bytes=60 * 1024 * 1024
        ),
        name="nested_basis",
    )(near_cols.T, near_count, far_cols.T, near_tiles, probes, mixing.T, far_tiles)


def solution(mesh):
    in_specs = (
        P("leaf", "blk", None, None),
        P("leaf", "blk"),
        P("leaf"),
        P("leaf", None, None),
        P(),
        P("leaf", "blk", None, None),
        P("leaf", "blk"),
    )
    out_specs = (P("leaf", "blk", None, None), P("leaf", None, None))
    return jax.shard_map(shards, mesh=mesh, in_specs=in_specs, out_specs=out_specs, check_vma=False)
```

```python
import functools
import math

import jax
import jax.numpy as jnp
from jax import lax
from jax.experimental import pallas as pl
from jax.experimental.pallas import tpu as pltpu
from jax.sharding import PartitionSpec as P

REACH = 8
MESH = pl.DeviceIdType.MESH
highest = lax.Precision.HIGHEST
f32 = jnp.float32
bf16 = jnp.bfloat16


def split_terms(value):
    high = value.astype(bf16)
    low = (value - high.astype(f32)).astype(bf16)
    return jnp.concatenate([high, low], axis=1)


def factor(gram):
    rank = gram.shape[0]
    rows = lax.broadcasted_iota(jnp.int32, (rank, 2 * rank), 0)
    lanes = lax.broadcasted_iota(jnp.int32, (rank, 2 * rank), 1)
    unit = jnp.where(lanes - rank == rows, 1.0, 0.0).astype(f32)
    work = jnp.where(lanes < rank, jnp.concatenate([gram, gram], axis=1), unit)
    done = []
    for start in range(0, rank, 8):
        index = lax.broadcasted_iota(jnp.int32, work.shape, 0)
        for step in range(0, 8, 2):
            j = start + step
            row_a = work[step : step + 1, :]
            row_b = work[step + 1 : step + 2, :]
            column_a = work[:, j : j + 1]
            column_b = work[:, j + 1 : j + 2]
            inverse_a = 1.0 / work[step : step + 1, j : j + 1]
            cross = work[step : step + 1, j + 1 : j + 2]
            ratio = cross * inverse_a
            inverse_b = 1.0 / (work[step + 1 : step + 2, j + 1 : j + 2] - cross * ratio)
            row_b = row_b - ratio * row_a
            column_b = column_b - ratio * column_a
            first = jnp.where(index > step, column_a * (row_a * inverse_a), 0.0)
            second = jnp.where(index > step + 1, column_b * (row_b * inverse_b), 0.0)
            work = work - first - second
        done.append(work[:8])
        work = work[8:] if start + 8 < rank else None
    full = jnp.concatenate(done, axis=0)
    pivots = jnp.sum(jnp.where(lanes == rows, full, 0.0), axis=1, keepdims=True)
    full = full / jnp.sqrt(pivots)
    upper = jnp.where(lanes >= rows, full, 0.0)[:, :rank]
    return upper, full[:, rank:]


def kernel(
    nl, nb, scale,
    cols_hbm, count_hbm, fcols_hbm, near_hbm, probes_hbm, mix_hbm, far_hbm,
    coup, root,
    cols, count, fcols, mix, pv, nv, fv, ywin, part, pair, sums, scat, gbuf, gleaf, ubuf, ball, front,
    pin, win, h_s, h_r, q_s, q_r, f_s, f_r, p_s, p_r, r_s, r_r, g_s, g_r, gl_s, gl_r,
    u_s, u_r, bm_s, bm_r, bz_s, bz_r, bl_s, bl_r, bx_s, bx_r,
):
    leaf = lax.axis_index("leaf")
    blk = lax.axis_index("blk")
    R = pv.shape[0]
    half = R // 2
    nz = nb // 2
    groups = nb // R
    size = pv.shape[1]
    rank = mix.shape[0]
    near_dev = nv.shape[1]
    far_dev = fv.shape[1]
    core = blk % 2
    own = blk % R
    z = own // 2
    base = blk - own
    mate = blk + 1 - 2 * core
    turn = (blk // 2) % 2
    beside = blk + 2 - 4 * turn
    quarter = half // 2
    pending = []

    def remote(src, dst, send, recv, to_leaf, to_blk):
        return pltpu.make_async_remote_copy(
            src_ref=src, dst_ref=dst, send_sem=send, recv_sem=recv,
            device_id=(to_leaf, to_blk), device_id_type=MESH,
        )

    order = [2 * (2 * m + turn) + core for m in range(quarter)]
    order += [2 * (2 * m + 1 - turn) + core for m in range(quarter)]
    order += [2 * k + 1 - core for k in range(half)]
    mix_load = pltpu.make_async_copy(mix_hbm, mix, win.at[2])
    mix_load.start()
    loads = [pltpu.make_async_copy(probes_hbm.at[i], pv.at[i], pin.at[k]) for k, i in enumerate(order)]
    near_load = pltpu.make_async_copy(near_hbm, nv, win.at[0])
    far_load = pltpu.make_async_copy(far_hbm, fv, win.at[1])
    small_loads = [
        pltpu.make_async_copy(cols_hbm, cols, win.at[3]),
        pltpu.make_async_copy(count_hbm, count, win.at[4]),
        pltpu.make_async_copy(fcols_hbm, fcols, win.at[5]),
    ]
    for load in loads + small_loads + [near_load, far_load]:
        load.start()

    barrier = pltpu.get_barrier_semaphore()
    for d in range(1, nl):
        pl.semaphore_signal(barrier, inc=1, device_id=((leaf + d) % nl, blk), device_id_type=MESH)
    for d in range(1, nb):
        pl.semaphore_signal(barrier, inc=1, device_id=(leaf, (blk + d) % nb), device_id_type=MESH)

    mix_load.wait()
    high = mix[...].astype(bf16).astype(f32)
    terms = jnp.concatenate([high, mix[...] - high], axis=0).T.astype(bf16)

    def mixed(i):
        product = jnp.dot(pv[i], terms, preferred_element_type=f32)
        ywin[R + i] = split_terms(product[:, :rank] + product[:, rank:])

    def over_leaf(side, m):
        i = 2 * (2 * m + turn) + core
        at = side * quarter + m
        to = (leaf + 1) % nl if side == 0 else (leaf + nl - 1) % nl
        return remote(ywin.at[R + i], ywin.at[2 * R * side + i], h_s.at[at], h_r.at[at], to, blk)

    def over_z(side, m, whose):
        i = 2 * R * side + 2 * (2 * m + whose) + core
        at = side * quarter + m
        return remote(ywin.at[i], ywin.at[i], q_s.at[at], q_r.at[at], leaf, beside)

    def share(side, k, parity):
        i = 2 * R * side + 2 * k + parity
        at = side * half + k
        return remote(ywin.at[i], ywin.at[i], f_s.at[at], f_r.at[at], leaf, mate)

    has_up = leaf < nl - 1
    has_down = leaf > 0
    sends = (has_up, has_down)
    gets = (has_down, has_up)
    for m in range(quarter):
        loads[m].wait()
        mixed(order[m])
        if m == 0:
            pl.semaphore_wait(barrier, nl - 1 + nb - 1)
        for side in range(2):

            @pl.when(sends[side])
            def _():
                over_leaf(side, m).start()

    for k in range(quarter, R):
        loads[k].wait()
        mixed(order[k])

    for side in range(2):

        @pl.when(jnp.logical_not(gets[side]))
        def _():
            ywin[2 * R * side : 2 * R * side + R] = jnp.zeros((R,) + ywin.shape[1:], bf16)

    for m in range(quarter):
        for side in range(2):

            @pl.when(gets[side])
            def _():
                over_leaf(side, m).wait_recv()
                over_z(side, m, turn).start()
                share(side, 2 * m + turn, core).start()

    for m in range(quarter):
        for side in range(2):

            @pl.when(gets[side])
            def _():
                over_z(side, m, 1 - turn).wait_recv()
                share(side, 2 * m + 1 - turn, core).start()

    for k in range(half):
        for side in range(2):

            @pl.when(gets[side])
            def _():
                share(side, k, 1 - core).wait_recv()

    for load in small_loads:
        load.wait()
    near_load.wait()

    def compressed(r):
        total = jnp.zeros((size, rank), f32)
        for s in range(near_dev):
            column = jnp.clip(cols[s, r] - (leaf - 1) * R, 0, 3 * R - 1)
            product = jnp.dot(nv[r, s], ywin[column], preferred_element_type=f32)
            live = blk * near_dev + s < count[r]
            total += jnp.where(live, product[:, :rank] + product[:, rank:], 0.0)
        return jnp.concatenate([total[: size // 2], total[size // 2 :]], axis=1)

    for k in range(half):
        part[k] = compressed(2 * k + 1 - core)
        copy = remote(part.at[k], pair.at[k], p_s.at[k], p_r.at[k], leaf, mate)
        copy.start()
        pending.append(copy)

    slot = blk // 2
    for k in range(half):
        mine = compressed(2 * k + core)
        pending[k].wait_recv()
        sums[k] = mine + pair[k]
        for g in range(groups):
            target = g * R + 2 * k + core

            @pl.when(target != blk)
            def _():
                remote(sums.at[k], scat.at[slot], r_s.at[k, g], r_r.at[slot], leaf, target).start()

            @pl.when(target == blk)
            def _():
                scat[slot] = sums[k]

    for d in range(1, nz):
        s = (slot + d) % nz
        remote(sums.at[0], scat.at[s], r_s.at[0, 0], r_r.at[s], leaf, mate).wait_recv()
    x = scat[0]
    for s in range(1, nz):
        x = x + scat[s]

    product = lax.dot_general(x, x, (((0,), (0,)), ((), ())), precision=highest, preferred_element_type=f32)
    gram = product[:rank, :rank] + product[rank:, rank:]
    gbuf[own] = gram
    for d in range(1, R):
        j = (own + d) % R
        copy = remote(gbuf.at[own], gbuf.at[own], g_s.at[d], g_r.at[own], leaf, base + j)
        copy.start()
        pending.append(copy)

    upper, inverse = factor(gram)
    zero = jnp.zeros((rank, rank), f32)
    twice = jnp.concatenate(
        [jnp.concatenate([inverse, zero], axis=1), jnp.concatenate([zero, inverse], axis=1)], axis=0
    )
    basis = lax.dot_general(x, twice, (((1,), (1,)), ((), ())), precision=highest, preferred_element_type=f32)

    def place(q_leaf, parity, q_z):
        return (q_leaf * 2 + parity) * half + q_z

    def spread(q_z):
        at = place(leaf, core, q_z)
        copies = [remote(ball.at[at], ball.at[at], bm_s.at[q_z], bm_r.at[q_z], leaf, mate)]
        for d in range(1, nl):
            copies.append(
                remote(
                    ball.at[at], ball.at[at], bl_s.at[d, q_z], bl_r.at[leaf, q_z], (leaf + d) % nl, blk
                )
            )
        for copy in copies:
            copy.start()
            pending.append(copy)

    def another(d):
        return (z // 2 + d // 2) % quarter * 2 + (z + d) % 2

    at = place(leaf, core, z)
    ball[at] = basis.astype(bf16)
    for d in range(1, half):
        to = another(d)
        copy = remote(ball.at[at], ball.at[at], bz_s.at[d], bz_r.at[z], leaf, base + 2 * to + core)
        copy.start()
        pending.append(copy)
    spread(z)
    ubuf[own] = upper
    for d in range(1, R):
        j = (own + d) % R
        copy = remote(ubuf.at[own], ubuf.at[own], u_s.at[d], u_r.at[own], leaf, base + j)
        copy.start()
        pending.append(copy)

    for d in range(1, R):
        j = (own + d) % R
        remote(gbuf.at[j], gbuf.at[j], g_s.at[d], g_r.at[j], leaf, mate).wait_recv()
    gram = gbuf[0]
    for j in range(1, R):
        gram = gram + gbuf[j]
    gleaf[leaf] = gram
    for d in range(1, nl):
        copy = remote(gleaf.at[leaf], gleaf.at[leaf], gl_s.at[d], gl_r.at[leaf], (leaf + d) % nl, blk)
        copy.start()
        pending.append(copy)

    def forward(d):
        other = another(d)
        at = place(leaf, core, other)
        remote(ball.at[at], ball.at[at], bz_s.at[d], bz_r.at[other], leaf, mate).wait_recv()
        spread(other)

    forward(1)
    for d in range(1, nl):
        s = (leaf + d) % nl
        remote(gleaf.at[s], gleaf.at[s], gl_s.at[d], gl_r.at[s], s, blk).wait_recv()
    gram = gleaf[0]
    for s in range(1, nl):
        gram = gram + gleaf[s]
    _, root_inverse = factor(gram)

    for d in range(2, half):
        forward(d)

    for k in range(half):
        at = place(leaf, 1 - core, k)
        remote(ball.at[at], ball.at[at], bm_s.at[k], bm_r.at[k], leaf, mate).wait_recv()
    far_load.wait()
    middle = size // 2
    for r in range(R):
        block = ball[place(leaf, r % 2, r // 2)]
        left = jnp.concatenate([block[:, :rank], block[:, rank:]], axis=0)
        for s in range(far_dev):
            image = lax.dot_general(
                left, fv[r, s], (((0,), (0,)), ((), ())), preferred_element_type=f32
            )
            high = image.astype(bf16)
            low = (image - high.astype(f32)).astype(bf16)
            front[r, s] = jnp.concatenate(
                [high[:, :middle], low[:, :middle], high[:, middle:], low[:, middle:]], axis=0
            )

    def relay(d):
        s = (leaf + nl - d) % nl
        for k in range(half):
            at = place(s, core, k)
            remote(ball.at[at], ball.at[at], bl_s.at[d, k], bl_r.at[s, k], s, blk).wait_recv()
        span = pl.ds(place(s, core, 0), half)
        copy = remote(ball.at[span], ball.at[span], bx_s.at[d], bx_r.at[s], leaf, mate)
        copy.start()
        pending.append(copy)

    for d in range(1, nl):
        relay(d)

    for d in range(1, R):
        j = (own + d) % R
        remote(ubuf.at[j], ubuf.at[j], u_s.at[d], u_r.at[j], leaf, mate).wait_recv()
    for r in range(R):
        root[r] = scale * lax.dot_general(
            ubuf[r], root_inverse, (((1,), (1,)), ((), ())), precision=highest, preferred_element_type=f32
        )

    for d in range(1, nl):
        s = (leaf + nl - d) % nl
        span = pl.ds(place(s, 1 - core, 0), half)
        remote(ball.at[span], ball.at[span], bx_s.at[d], bx_r.at[s], leaf, mate).wait_recv()

    for r in range(R):
        for s in range(far_dev):
            q = fcols[s, r]
            block = ball[place(q // R, q % 2, (q % R) // 2)]
            product = jnp.dot(front[r, s], block, preferred_element_type=f32)
            upper = product[:rank] + product[rank : 2 * rank]
            lower = product[2 * rank : 3 * rank] + product[3 * rank :]
            coup[r, s] = upper[:, :rank] + lower[:, rank:]

    for copy in pending:
        copy.wait_send()
    for side in range(2):
        for m in range(quarter):

            @pl.when(sends[side])
            def _():
                over_leaf(side, m).wait_send()

            @pl.when(gets[side])
            def _():
                over_z(side, m, turn).wait_send()

        for k in range(half):

            @pl.when(gets[side])
            def _():
                share(side, k, core).wait_send()

    for k in range(half):
        for g in range(groups):
            target = g * R + 2 * k + core

            @pl.when(target != blk)
            def _():
                remote(sums.at[k], scat.at[slot], r_s.at[k, g], r_r.at[slot], leaf, target).wait_send()


def shards(near_tiles, near_cols, near_count, probes, mixing, far_tiles, far_cols):
    nl, nb = lax.axis_size("leaf"), lax.axis_size("blk")
    R, size, width = probes.shape
    rank = mixing.shape[1]
    half, nz, groups = R // 2, nb // 2, nb // R
    assert R % 4 == 0 and nb % R == 0 and REACH <= R and nl > 1
    dma = pltpu.SemaphoreType.DMA
    packed = (size // 2, 2 * rank)
    vmem = pl.BlockSpec(memory_space=pltpu.VMEM)
    hbm = pl.BlockSpec(memory_space=pltpu.HBM)
    scale = math.sqrt(nl * R * rank)
    return pl.pallas_call(
        functools.partial(kernel, nl, nb, scale),
        out_shape=(
            jax.ShapeDtypeStruct((R, far_tiles.shape[1], rank, rank), f32),
            jax.ShapeDtypeStruct((R, rank, rank), f32),
        ),
        in_specs=[hbm] * 7,
        out_specs=(vmem, vmem),
        scratch_shapes=[
            pltpu.SMEM(near_cols.shape[::-1], jnp.int32),
            pltpu.SMEM(near_count.shape, jnp.int32),
            pltpu.SMEM(far_cols.shape[::-1], jnp.int32),
            pltpu.VMEM(mixing.shape[::-1], f32),
            pltpu.VMEM(probes.shape, bf16),
            pltpu.VMEM(near_tiles.shape, bf16),
            pltpu.VMEM(far_tiles.shape, bf16),
            pltpu.VMEM((3 * R, size, 2 * rank), bf16),
            pltpu.VMEM((half,) + packed, f32),
            pltpu.VMEM((half,) + packed, f32),
            pltpu.VMEM((half,) + packed, f32),
            pltpu.VMEM((nz,) + packed, f32),
            pltpu.VMEM((R, rank, rank), f32),
            pltpu.VMEM((nl, rank, rank), f32),
            pltpu.VMEM((R, rank, rank), f32),
            pltpu.VMEM((nl * R,) + packed, bf16),
            pltpu.VMEM((R, far_tiles.shape[1], 4 * rank, size // 2), bf16),
            dma((R,)), dma((6,)),
            dma((half,)), dma((half,)), dma((half,)), dma((half,)), dma((R,)), dma((R,)),
            dma((half,)), dma((half,)),
            dma((half, groups)), dma((nz,)),
            dma((R,)), dma((R,)), dma((nl,)), dma((nl,)),
            dma((R,)), dma((R,)), dma((half,)), dma((half,)),
            dma((half,)), dma((half,)),
            dma((nl, half)), dma((nl, half)), dma((nl,)), dma((nl,)),
        ],
        compiler_params=pltpu.CompilerParams(
            collective_id=0, has_side_effects=True, vmem_limit_bytes=52 * 1024 * 1024
        ),
        name="nested_basis",
    )(near_cols.T, near_count, far_cols.T, near_tiles, probes, mixing.T, far_tiles)


def solution(mesh):
    in_specs = (
        P("leaf", "blk", None, None),
        P("leaf", "blk"),
        P("leaf"),
        P("leaf", None, None),
        P(),
        P("leaf", "blk", None, None),
        P("leaf", "blk"),
    )
    out_specs = (P("leaf", "blk", None, None), P("leaf", None, None))
    return jax.shard_map(shards, mesh=mesh, in_specs=in_specs, out_specs=out_specs, check_vma=False)
```

```python
import functools
import math

import jax
import jax.numpy as jnp
from jax import lax
from jax.experimental import pallas as pl
from jax.experimental.pallas import tpu as pltpu
from jax.sharding import PartitionSpec as P

REACH = 8
MESH = pl.DeviceIdType.MESH
highest = lax.Precision.HIGHEST
f32 = jnp.float32
bf16 = jnp.bfloat16


def split_terms(value):
    high = value.astype(bf16)
    low = (value - high.astype(f32)).astype(bf16)
    return jnp.concatenate([high, low], axis=1)


def factor(gram):
    rank = gram.shape[0]
    rows = lax.broadcasted_iota(jnp.int32, (rank, 2 * rank), 0)
    lanes = lax.broadcasted_iota(jnp.int32, (rank, 2 * rank), 1)
    unit = jnp.where(lanes - rank == rows, 1.0, 0.0).astype(f32)
    work = jnp.where(lanes < rank, jnp.concatenate([gram, gram], axis=1), unit)
    done = []
    for start in range(0, rank, 8):
        index = lax.broadcasted_iota(jnp.int32, work.shape, 0)
        for step in range(0, 8, 2):
            j = start + step
            row_a = work[step : step + 1, :]
            row_b = work[step + 1 : step + 2, :]
            column_a = work[:, j : j + 1]
            column_b = work[:, j + 1 : j + 2]
            inverse_a = 1.0 / work[step : step + 1, j : j + 1]
            cross = work[step : step + 1, j + 1 : j + 2]
            ratio = cross * inverse_a
            inverse_b = 1.0 / (work[step + 1 : step + 2, j + 1 : j + 2] - cross * ratio)
            row_b = row_b - ratio * row_a
            column_b = column_b - ratio * column_a
            first = jnp.where(index > step, column_a * (row_a * inverse_a), 0.0)
            second = jnp.where(index > step + 1, column_b * (row_b * inverse_b), 0.0)
            work = work - first - second
        done.append(work[:8])
        work = work[8:] if start + 8 < rank else None
    full = jnp.concatenate(done, axis=0)
    pivots = jnp.sum(jnp.where(lanes == rows, full, 0.0), axis=1, keepdims=True)
    full = full / jnp.sqrt(pivots)
    upper = jnp.where(lanes >= rows, full, 0.0)[:, :rank]
    return upper, full[:, rank:]


def kernel(
    nl, nb, scale,
    cols_hbm, count_hbm, fcols_hbm, near_hbm, probes_hbm, mix_hbm, far_hbm,
    coup, root,
    cols, count, fcols, mix, pv, nv, fv, ywin, part, pair, sums, scat, gbuf, gleaf, ubuf, ball, front,
    pin, win, h_s, h_r, q_s, q_r, f_s, f_r, p_s, p_r, r_s, r_r, g_s, g_r, gl_s, gl_r,
    u_s, u_r, bm_s, bm_r, bz_s, bz_r, bl_s, bl_r, bx_s, bx_r,
):
    leaf = lax.axis_index("leaf")
    blk = lax.axis_index("blk")
    R = pv.shape[0]
    half = R // 2
    nz = nb // 2
    groups = nb // R
    size = pv.shape[1]
    rank = mix.shape[0]
    near_dev = nv.shape[1]
    far_dev = fv.shape[1]
    core = blk % 2
    own = blk % R
    z = own // 2
    base = blk - own
    mate = blk + 1 - 2 * core
    turn = (blk // 2) % 2
    beside = blk + 2 - 4 * turn
    quarter = half // 2
    pending = []

    def remote(src, dst, send, recv, to_leaf, to_blk):
        return pltpu.make_async_remote_copy(
            src_ref=src, dst_ref=dst, send_sem=send, recv_sem=recv,
            device_id=(to_leaf, to_blk), device_id_type=MESH,
        )

    order = [2 * (2 * m + turn) + core for m in range(quarter)]
    order += [2 * (2 * m + 1 - turn) + core for m in range(quarter)]
    order += [2 * k + 1 - core for k in range(half)]
    mix_load = pltpu.make_async_copy(mix_hbm, mix, win.at[2])
    mix_load.start()
    loads = [pltpu.make_async_copy(probes_hbm.at[i], pv.at[i], pin.at[k]) for k, i in enumerate(order)]
    near_load = pltpu.make_async_copy(near_hbm, nv, win.at[0])
    far_load = pltpu.make_async_copy(far_hbm, fv, win.at[1])
    small_loads = [
        pltpu.make_async_copy(cols_hbm, cols, win.at[3]),
        pltpu.make_async_copy(count_hbm, count, win.at[4]),
        pltpu.make_async_copy(fcols_hbm, fcols, win.at[5]),
    ]
    for load in loads + small_loads + [near_load, far_load]:
        load.start()

    barrier = pltpu.get_barrier_semaphore()
    for d in range(1, nl):
        pl.semaphore_signal(barrier, inc=1, device_id=((leaf + d) % nl, blk), device_id_type=MESH)
    for d in range(1, nb):
        pl.semaphore_signal(barrier, inc=1, device_id=(leaf, (blk + d) % nb), device_id_type=MESH)

    mix_load.wait()
    high = mix[...].astype(bf16).astype(f32)
    terms = jnp.concatenate([high, mix[...] - high], axis=0).T.astype(bf16)

    def mixed(i):
        product = jnp.dot(pv[i], terms, preferred_element_type=f32)
        ywin[R + i] = split_terms(product[:, :rank] + product[:, rank:])

    def over_leaf(side, m):
        i = 2 * (2 * m + turn) + core
        at = side * quarter + m
        to = (leaf + 1) % nl if side == 0 else (leaf + nl - 1) % nl
        return remote(ywin.at[R + i], ywin.at[2 * R * side + i], h_s.at[at], h_r.at[at], to, blk)

    def over_z(side, m, whose):
        i = 2 * R * side + 2 * (2 * m + whose) + core
        at = side * quarter + m
        return remote(ywin.at[i], ywin.at[i], q_s.at[at], q_r.at[at], leaf, beside)

    def share(side, k, parity):
        i = 2 * R * side + 2 * k + parity
        at = side * half + k
        return remote(ywin.at[i], ywin.at[i], f_s.at[at], f_r.at[at], leaf, mate)

    has_up = leaf < nl - 1
    has_down = leaf > 0
    sends = (has_up, has_down)
    gets = (has_down, has_up)
    for m in range(quarter):
        loads[m].wait()
        mixed(order[m])
        if m == 0:
            pl.semaphore_wait(barrier, nl - 1 + nb - 1)
        for side in range(2):

            @pl.when(sends[side])
            def _():
                over_leaf(side, m).start()

    for k in range(quarter, R):
        loads[k].wait()
        mixed(order[k])

    for side in range(2):

        @pl.when(jnp.logical_not(gets[side]))
        def _():
            ywin[2 * R * side : 2 * R * side + R] = jnp.zeros((R,) + ywin.shape[1:], bf16)

    for m in range(quarter):
        for side in range(2):

            @pl.when(gets[side])
            def _():
                over_leaf(side, m).wait_recv()
                over_z(side, m, turn).start()
                share(side, 2 * m + turn, core).start()

    for m in range(quarter):
        for side in range(2):

            @pl.when(gets[side])
            def _():
                over_z(side, m, 1 - turn).wait_recv()
                share(side, 2 * m + 1 - turn, core).start()

    for k in range(half):
        for side in range(2):

            @pl.when(gets[side])
            def _():
                share(side, k, 1 - core).wait_recv()

    for load in small_loads:
        load.wait()
    near_load.wait()

    def compressed(r):
        total = jnp.zeros((size, rank), f32)
        for s in range(near_dev):
            column = jnp.clip(cols[s, r] - (leaf - 1) * R, 0, 3 * R - 1)
            product = jnp.dot(nv[r, s], ywin[column], preferred_element_type=f32)
            live = blk * near_dev + s < count[r]
            total += jnp.where(live, product[:, :rank] + product[:, rank:], 0.0)
        return jnp.concatenate([total[: size // 2], total[size // 2 :]], axis=1)

    for k in range(half):
        part[k] = compressed(2 * k + 1 - core)
        copy = remote(part.at[k], pair.at[k], p_s.at[k], p_r.at[k], leaf, mate)
        copy.start()
        pending.append(copy)

    slot = blk // 2
    for k in range(half):
        mine = compressed(2 * k + core)
        pending[k].wait_recv()
        sums[k] = mine + pair[k]
        for g in range(groups):
            target = g * R + 2 * k + core

            @pl.when(target != blk)
            def _():
                remote(sums.at[k], scat.at[slot], r_s.at[k, g], r_r.at[slot], leaf, target).start()

            @pl.when(target == blk)
            def _():
                scat[slot] = sums[k]

    for d in range(1, nz):
        s = (slot + d) % nz
        remote(sums.at[0], scat.at[s], r_s.at[0, 0], r_r.at[s], leaf, mate).wait_recv()
    x = scat[0]
    for s in range(1, nz):
        x = x + scat[s]

    product = lax.dot_general(x, x, (((0,), (0,)), ((), ())), precision=highest, preferred_element_type=f32)
    gram = product[:rank, :rank] + product[rank:, rank:]
    gbuf[own] = gram
    for d in range(1, R):
        j = (own + d) % R
        copy = remote(gbuf.at[own], gbuf.at[own], g_s.at[d], g_r.at[own], leaf, base + j)
        copy.start()
        pending.append(copy)

    upper, inverse = factor(gram)
    zero = jnp.zeros((rank, rank), f32)
    twice = jnp.concatenate(
        [jnp.concatenate([inverse, zero], axis=1), jnp.concatenate([zero, inverse], axis=1)], axis=0
    )
    basis = lax.dot_general(x, twice, (((1,), (1,)), ((), ())), precision=highest, preferred_element_type=f32)

    def place(q_leaf, parity, q_z):
        return (q_leaf * 2 + parity) * half + q_z

    def spread(q_z):
        at = place(leaf, core, q_z)
        copies = [remote(ball.at[at], ball.at[at], bm_s.at[q_z], bm_r.at[q_z], leaf, mate)]
        for d in range(1, nl):
            copies.append(
                remote(
                    ball.at[at], ball.at[at], bl_s.at[d, q_z], bl_r.at[leaf, q_z], (leaf + d) % nl, blk
                )
            )
        for copy in copies:
            copy.start()
            pending.append(copy)

    def another(d):
        return (z // 2 + d // 2) % quarter * 2 + (z + d) % 2

    at = place(leaf, core, z)
    ball[at] = basis.astype(bf16)
    for d in range(1, half):
        to = another(d)
        copy = remote(ball.at[at], ball.at[at], bz_s.at[d], bz_r.at[z], leaf, base + 2 * to + core)
        copy.start()
        pending.append(copy)
    spread(z)
    ubuf[own] = upper
    for d in range(1, R):
        j = (own + d) % R
        copy = remote(ubuf.at[own], ubuf.at[own], u_s.at[d], u_r.at[own], leaf, base + j)
        copy.start()
        pending.append(copy)

    for d in range(1, R):
        j = (own + d) % R
        remote(gbuf.at[j], gbuf.at[j], g_s.at[d], g_r.at[j], leaf, mate).wait_recv()
    gram = gbuf[0]
    for j in range(1, R):
        gram = gram + gbuf[j]
    gleaf[leaf] = gram
    for d in range(1, nl):
        copy = remote(gleaf.at[leaf], gleaf.at[leaf], gl_s.at[d], gl_r.at[leaf], (leaf + d) % nl, blk)
        copy.start()
        pending.append(copy)

    def forward(d):
        other = another(d)
        at = place(leaf, core, other)
        remote(ball.at[at], ball.at[at], bz_s.at[d], bz_r.at[other], leaf, mate).wait_recv()
        spread(other)

    forward(1)
    for d in range(2, half):
        forward(d)

    for k in range(half):
        at = place(leaf, 1 - core, k)
        remote(ball.at[at], ball.at[at], bm_s.at[k], bm_r.at[k], leaf, mate).wait_recv()
    far_load.wait()
    middle = size // 2
    for r in range(R):
        block = ball[place(leaf, r % 2, r // 2)]
        left = jnp.concatenate([block[:, :rank], block[:, rank:]], axis=0)
        for s in range(far_dev):
            image = lax.dot_general(
                left, fv[r, s], (((0,), (0,)), ((), ())), preferred_element_type=f32
            )
            high = image.astype(bf16)
            low = (image - high.astype(f32)).astype(bf16)
            front[r, s] = jnp.concatenate(
                [high[:, :middle], low[:, :middle], high[:, middle:], low[:, middle:]], axis=0
            )

    def relay(d):
        s = (leaf + nl - d) % nl
        for k in range(half):
            at = place(s, core, k)
            remote(ball.at[at], ball.at[at], bl_s.at[d, k], bl_r.at[s, k], s, blk).wait_recv()
        span = pl.ds(place(s, core, 0), half)
        copy = remote(ball.at[span], ball.at[span], bx_s.at[d], bx_r.at[s], leaf, mate)
        copy.start()
        pending.append(copy)

    for d in range(1, nl):
        s = (leaf + d) % nl
        remote(gleaf.at[s], gleaf.at[s], gl_s.at[d], gl_r.at[s], s, blk).wait_recv()
    gram = gleaf[0]
    for s in range(1, nl):
        gram = gram + gleaf[s]
    _, root_inverse = factor(gram)

    for d in range(1, nl):
        relay(d)

    for d in range(1, R):
        j = (own + d) % R
        remote(ubuf.at[j], ubuf.at[j], u_s.at[d], u_r.at[j], leaf, mate).wait_recv()
    for r in range(R):
        root[r] = scale * lax.dot_general(
            ubuf[r], root_inverse, (((1,), (1,)), ((), ())), precision=highest, preferred_element_type=f32
        )

    for d in range(1, nl):
        s = (leaf + nl - d) % nl
        span = pl.ds(place(s, 1 - core, 0), half)
        remote(ball.at[span], ball.at[span], bx_s.at[d], bx_r.at[s], leaf, mate).wait_recv()

    for r in range(R):
        for s in range(far_dev):
            q = fcols[s, r]
            block = ball[place(q // R, q % 2, (q % R) // 2)]
            product = jnp.dot(front[r, s], block, preferred_element_type=f32)
            upper = product[:rank] + product[rank : 2 * rank]
            lower = product[2 * rank : 3 * rank] + product[3 * rank :]
            coup[r, s] = upper[:, :rank] + lower[:, rank:]

    for copy in pending:
        copy.wait_send()
    for side in range(2):
        for m in range(quarter):

            @pl.when(sends[side])
            def _():
                over_leaf(side, m).wait_send()

            @pl.when(gets[side])
            def _():
                over_z(side, m, turn).wait_send()

        for k in range(half):

            @pl.when(gets[side])
            def _():
                share(side, k, core).wait_send()

    for k in range(half):
        for g in range(groups):
            target = g * R + 2 * k + core

            @pl.when(target != blk)
            def _():
                remote(sums.at[k], scat.at[slot], r_s.at[k, g], r_r.at[slot], leaf, target).wait_send()


def shards(near_tiles, near_cols, near_count, probes, mixing, far_tiles, far_cols):
    nl, nb = lax.axis_size("leaf"), lax.axis_size("blk")
    R, size, width = probes.shape
    rank = mixing.shape[1]
    half, nz, groups = R // 2, nb // 2, nb // R
    assert R % 4 == 0 and nb % R == 0 and REACH <= R and nl > 1
    dma = pltpu.SemaphoreType.DMA
    packed = (size // 2, 2 * rank)
    vmem = pl.BlockSpec(memory_space=pltpu.VMEM)
    hbm = pl.BlockSpec(memory_space=pltpu.HBM)
    scale = math.sqrt(nl * R * rank)
    return pl.pallas_call(
        functools.partial(kernel, nl, nb, scale),
        out_shape=(
            jax.ShapeDtypeStruct((R, far_tiles.shape[1], rank, rank), f32),
            jax.ShapeDtypeStruct((R, rank, rank), f32),
        ),
        in_specs=[hbm] * 7,
        out_specs=(vmem, vmem),
        scratch_shapes=[
            pltpu.SMEM(near_cols.shape[::-1], jnp.int32),
            pltpu.SMEM(near_count.shape, jnp.int32),
            pltpu.SMEM(far_cols.shape[::-1], jnp.int32),
            pltpu.VMEM(mixing.shape[::-1], f32),
            pltpu.VMEM(probes.shape, bf16),
            pltpu.VMEM(near_tiles.shape, bf16),
            pltpu.VMEM(far_tiles.shape, bf16),
            pltpu.VMEM((3 * R, size, 2 * rank), bf16),
            pltpu.VMEM((half,) + packed, f32),
            pltpu.VMEM((half,) + packed, f32),
            pltpu.VMEM((half,) + packed, f32),
            pltpu.VMEM((nz,) + packed, f32),
            pltpu.VMEM((R, rank, rank), f32),
            pltpu.VMEM((nl, rank, rank), f32),
            pltpu.VMEM((R, rank, rank), f32),
            pltpu.VMEM((nl * R,) + packed, bf16),
            pltpu.VMEM((R, far_tiles.shape[1], 4 * rank, size // 2), bf16),
            dma((R,)), dma((6,)),
            dma((half,)), dma((half,)), dma((half,)), dma((half,)), dma((R,)), dma((R,)),
            dma((half,)), dma((half,)),
            dma((half, groups)), dma((nz,)),
            dma((R,)), dma((R,)), dma((nl,)), dma((nl,)),
            dma((R,)), dma((R,)), dma((half,)), dma((half,)),
            dma((half,)), dma((half,)),
            dma((nl, half)), dma((nl, half)), dma((nl,)), dma((nl,)),
        ],
        compiler_params=pltpu.CompilerParams(
            collective_id=0, has_side_effects=True, vmem_limit_bytes=60 * 1024 * 1024
        ),
        name="nested_basis",
    )(near_cols.T, near_count, far_cols.T, near_tiles, probes, mixing.T, far_tiles)


def solution(mesh):
    in_specs = (
        P("leaf", "blk", None, None),
        P("leaf", "blk"),
        P("leaf"),
        P("leaf", None, None),
        P(),
        P("leaf", "blk", None, None),
        P("leaf", "blk"),
    )
    out_specs = (P("leaf", "blk", None, None), P("leaf", None, None))
    return jax.shard_map(shards, mesh=mesh, in_specs=in_specs, out_specs=out_specs, check_vma=False)
```
